32 devices in a mesh: parts: 2 (over x), blk: 16 (over z, y, core).
Axes of the slice: x: 2, y: 2, z: 4, core: 2. Of those that a mesh axis runs over, the one named last changes fastest.
Arguments:
- embeddings: bfloat16 [32768, 1024], P(('parts', 'blk')), parts along dimension 0, may hold values from -256 to 256
- owner_ids: int32 [32768, 1], P(('parts', 'blk')), parts along dimension 0, may hold values from 0 to 15, as said below
- local_cluster: int32 [32768], P(('parts', 'blk')), parts along dimension 0, may hold values from 0 to 63
- arrival_rank: int32 [32768], P(('parts', 'blk')), parts along dimension 0, may hold values from 0 to 16383, each once
Outputs:
- scores: float32 [32768], P(('parts', 'blk')), parts along dimension 0
The draws below stay inside these ranges and needn't reach their ends.
There are 2 independent parts, one for each index of `parts`. The reference program is written for one: setup_inputs(seed, part) draws one part's arguments, and reference() takes and returns one part's arrays. A program takes and returns all parts, laid end to end along the dimension named above; each array names one. Nothing has to cross between parts.
Inputs may be any that keep to these rules, and one draw needn't show every extreme that they name: `owner_ids`: in each aligned block of 1024 rows (the rows of one device) no owner is named by more than 128 rows; one owner is named by exactly 128 rows in every block. `arrival_rank`: each of 0 to 16383 appears once.
All inputs are finite; a program needn't handle non-finite values.
Results may differ from the reference program's by a relative error of at most 0.00033.
Values may be sent and summed in bfloat16 or wider, within the bound.
A program may use at most 64 MiB of HBM per device.

```python
import math
import jax
import jax.numpy as jnp
from jax import lax

D = 1024
ENTRIES_PER_CHIP = 1024
CL_DEV = 64
TOKENS = 16384
CAP = 128
N_BLK = 16


def cluster_layout(key):
    bias_key, base_key, pick_key, order_key, lookup_random_seed, first_key, second_key = jax.random.split(key, 7)
    slot_count = 2 * ENTRIES_PER_CHIP
    owner_bias = jax.random.randint(bias_key, (N_BLK,), 0, 8192, dtype=jnp.int32)
    favored = jax.random.randint(pick_key, (), 0, N_BLK, dtype=jnp.int32)
    owner_bias = jnp.where(jnp.arange(N_BLK, dtype=jnp.int32) == favored, 32768, owner_bias).astype(jnp.int32)
    slot_owner = jnp.arange(slot_count, dtype=jnp.int32) // CAP
    base_draw = jax.random.randint(base_key, (N_BLK, slot_count), 0, 8192, dtype=jnp.int32)
    slot_score = (base_draw + owner_bias[slot_owner][None, :]) * slot_count + jnp.arange(slot_count, dtype=jnp.int32)[None, :]
    chosen = jnp.argsort(-slot_score, axis=1)[:, :ENTRIES_PER_CHIP]
    picked = (chosen // CAP).astype(jnp.int32)
    order_draw = jax.random.randint(order_key, (N_BLK, ENTRIES_PER_CHIP), 0, 1 << 20, dtype=jnp.int32) * ENTRIES_PER_CHIP + jnp.arange(ENTRIES_PER_CHIP, dtype=jnp.int32)[None, :]
    row_order = jnp.argsort(order_draw, axis=1)
    owners = jnp.take_along_axis(picked, row_order, axis=1).reshape(TOKENS).astype(jnp.int32)
    table_draw = jax.random.randint(lookup_random_seed, (N_BLK, CL_DEV), 0, 1 << 20, dtype=jnp.int32) * CL_DEV + jnp.arange(CL_DEV, dtype=jnp.int32)[None, :]
    relabel = jnp.argsort(table_draw, axis=1).astype(jnp.int32)
    first_draw = jax.random.randint(first_key, (TOKENS,), 0, CL_DEV, dtype=jnp.int32)
    second_draw = jax.random.randint(second_key, (TOKENS,), 0, CL_DEV, dtype=jnp.int32)
    raw_rank = jnp.minimum(first_draw, second_draw)
    local_ids = relabel[owners, raw_rank].astype(jnp.int32)
    return (owners, local_ids)


def draw_owner_ids(key, part):
    owners, local_ids = cluster_layout(key)
    return owners.reshape(TOKENS, 1)


def draw_local_cluster(key, part):
    owners, local_ids = cluster_layout(key)
    return local_ids


def draw_embeddings(key, part):
    owners, local_ids = cluster_layout(key)
    key = jax.random.fold_in(key, 11)
    center_key, pull_key, seed_key, flag_key, noise_key, scale_key = jax.random.split(key, 6)
    cluster_total = N_BLK * CL_DEV
    cluster = owners * CL_DEV + local_ids
    centers = jnp.clip(jax.random.normal(center_key, (cluster_total, D), jnp.float32), -4.0, 4.0)
    cluster_pull = jnp.exp(jax.random.uniform(pull_key, (cluster_total,), jnp.float32, 0.0, math.log(3.0)))
    dup_seeds = jnp.clip(jax.random.normal(seed_key, (2 * cluster_total, D), jnp.float32), -4.0, 4.0)
    dup_flag = jax.random.randint(flag_key, (TOKENS,), 0, 16, dtype=jnp.int32)
    row_noise = jnp.clip(jax.random.normal(noise_key, (TOKENS, D), jnp.float32), -4.0, 4.0)
    scales = jnp.exp(jax.random.uniform(scale_key, (TOKENS, 1), jnp.float32, 0.0, math.log(10.0)))
    spread = 0.15
    is_copy = dup_flag < 2
    seed_rows = dup_seeds[cluster * 2 + jnp.minimum(dup_flag, 1)]
    centered = cluster_pull[cluster][:, None] * centers[cluster]
    row_values = jnp.where(is_copy[:, None], centered + seed_rows + spread * row_noise, centered + row_noise)
    return jnp.clip(scales * row_values, -256.0, 256.0).astype(jnp.bfloat16)


def setup_inputs(seed: int = 0, part: int = 0) -> dict:
    splits = jax.random.split(jax.random.key(seed), 5)
    part_splits = jax.random.split(jax.random.fold_in(splits[4], part), 5)
    embeddings = draw_embeddings(jax.random.fold_in(jax.random.fold_in(splits[4], part), 71), part)
    owner_ids = draw_owner_ids(jax.random.fold_in(jax.random.fold_in(splits[4], part), 71), part)
    local_cluster = draw_local_cluster(jax.random.fold_in(jax.random.fold_in(splits[4], part), 71), part)
    arrival_rank = jax.random.permutation(part_splits[3], TOKENS).astype(jnp.int32)
    return {"embeddings": embeddings, "owner_ids": owner_ids, "local_cluster": local_cluster, "arrival_rank": arrival_rank}


sharpness_divisor = 0.05

def reference(embeddings, owner_ids, local_cluster, arrival_rank):
    all_rows = embeddings.shape[0]
    wide_rows = embeddings.astype(jnp.float32)
    unit_rows = (wide_rows / jnp.sqrt(lax.optimization_barrier(jnp.sum(wide_rows * wide_rows, axis=1, keepdims=True)) + 1e-06)).astype(jnp.bfloat16)
    cluster = (owner_ids[:, 0] * CL_DEV + local_cluster).astype(jnp.int32)
    sort_key = (cluster * all_rows + arrival_rank).astype(jnp.int32)
    sorted_index = jnp.argsort(sort_key, stable=True).astype(jnp.int32)
    sorted_rows = unit_rows[sorted_index]
    sorted_keys = sort_key[sorted_index]
    sorted_groups = cluster[sorted_index]
    lookback = 2 * ENTRIES_PER_CHIP
    block_rows = min(512, all_rows)
    padded_rows = jnp.concatenate([jnp.zeros((lookback, embeddings.shape[1]), jnp.bfloat16), sorted_rows], axis=0)
    filled_key_rows = jnp.concatenate([jnp.full((lookback,), -1, jnp.int32), sorted_keys.astype(jnp.int32)], axis=0)
    padded_groups = jnp.concatenate([jnp.full((lookback,), -1, jnp.int32), sorted_groups.astype(jnp.int32)], axis=0)

    def block_scores(block_number):
        first_row = (block_number * block_rows).astype(jnp.int32)
        row_units = lax.dynamic_slice_in_dim(sorted_rows, first_row, block_rows, 0)
        key_rows_local = lax.dynamic_slice_in_dim(sorted_keys.astype(jnp.int32), first_row, block_rows, 0)
        row_groups = lax.dynamic_slice_in_dim(sorted_groups.astype(jnp.int32), first_row, block_rows, 0)
        col_units = lax.dynamic_slice_in_dim(padded_rows, first_row, lookback + block_rows, 0)
        col_keys = lax.dynamic_slice_in_dim(filled_key_rows, first_row, lookback + block_rows, 0)
        col_groups = lax.dynamic_slice_in_dim(padded_groups, first_row, lookback + block_rows, 0)
        inner_dot_values = jnp.dot(row_units, col_units.T, preferred_element_type=jnp.float32)
        pairing_factors = (col_groups[None, :] == row_groups[:, None]) & (col_keys[None, :] < key_rows_local[:, None])
        return lax.optimization_barrier(jnp.sum(jnp.where(pairing_factors, jnp.exp(inner_dot_values / sharpness_divisor), jnp.zeros_like(inner_dot_values)), axis=1))
    totals = lax.map(block_scores, jnp.arange(all_rows // block_rows, dtype=jnp.int32))
    sorted_scores = jnp.log1p(totals.reshape(-1))
    return jnp.zeros((all_rows,), sorted_scores.dtype).at[sorted_index].set(sorted_scores)
```

```python
import functools

import jax
import jax.numpy as jnp
from jax import lax
from jax.experimental import pallas as pl
from jax.experimental.pallas import tpu as pltpu
from jax.sharding import PartitionSpec as P

CL_DEV = 64
SLOTS = 128
PAIR = 2 * SLOTS
SHARPNESS = 20.0 * 1.4426950408889634


def dot_nt(a, b):
    return lax.dot_general(a, b, (((1,), (1,)), ((), ())), preferred_element_type=jnp.float32)


def kernel(
    n, emb, tgt, lc, rank, out,
    unit, send, recv, ksend, krecv, rowacc, ssend, ret,
    us, ur, ks, kr, rs, rr,
):
    rows = emb.shape[0]
    all_rows = rows * n
    nc = n // 2
    me = lax.axis_index("blk")
    mine = me // 2
    mate = me + 1 - 2 * (me % 2)

    barrier = pltpu.get_barrier_semaphore()

    def greet(k, _):
        pl.semaphore_signal(
            barrier, inc=1, device_id={"blk": (me + k) % n}, device_id_type=pl.DeviceIdType.MESH
        )
        return 0

    lax.fori_loop(1, n, greet, 0)

    def normalise(i, _):
        span = pl.ds(pl.multiple_of(i * 128, 128), 128)
        wide = emb[span, :].astype(jnp.float32)
        inv = 1.0 / jnp.sqrt(jnp.sum(wide * wide, axis=1, keepdims=True) + 1e-06)
        unit[span, :] = (wide * inv).astype(jnp.bfloat16)
        return 0

    lax.fori_loop(0, rows // 128, normalise, 0)

    target = tgt[...]
    hits = target == lax.broadcasted_iota(jnp.int32, (n, rows), 0)
    before = (
        lax.broadcasted_iota(jnp.int32, (rows, rows), 0)
        < lax.broadcasted_iota(jnp.int32, (rows, rows), 1)
    )
    hits_f = hits.astype(jnp.float32)
    earlier = jnp.dot(
        hits_f.astype(jnp.bfloat16),
        before.astype(jnp.float32).astype(jnp.bfloat16),
        preferred_element_type=jnp.float32,
    )
    pos = jnp.sum(hits_f * earlier, axis=0, keepdims=True).astype(jnp.int32)
    slot = target * SLOTS + pos
    at_slot = pos == lax.broadcasted_iota(jnp.int32, (SLOTS, rows), 0)
    at_slot_b = at_slot.astype(jnp.float32).astype(jnp.bfloat16)

    rank_v = rank[...]
    rank_hi = rank_v // 256
    rank_lo = rank_v - rank_hi * 256
    parts = [
        hits_f,
        hits_f * lc[...].astype(jnp.float32),
        hits_f * rank_hi.astype(jnp.float32),
        hits_f * rank_lo.astype(jnp.float32),
    ]
    table = [dot_nt(p.astype(jnp.bfloat16), at_slot_b) for p in parts]
    base = (table[1] + (1.0 - table[0]) * float(CL_DEV)) * float(all_rows)
    key = base + table[2] * 256.0 + table[3]
    top = lax.broadcasted_iota(jnp.int32, (n, 8, SLOTS), 1) < 4
    ksend[...] = jnp.where(top, key[:, None, :], base[:, None, :])

    def key_copy(src, dst, send_at, recv_at, dev):
        return pltpu.make_async_remote_copy(
            src_ref=ksend.at[src], dst_ref=krecv.at[dst],
            send_sem=ks.at[send_at], recv_sem=kr.at[recv_at],
            device_id={"blk": dev}, device_id_type=pl.DeviceIdType.MESH,
        )

    def unit_copy(src, dst, send_at, recv_at, dev):
        return pltpu.make_async_remote_copy(
            src_ref=send.at[src], dst_ref=recv.at[dst],
            send_sem=us.at[send_at], recv_sem=ur.at[recv_at],
            device_id={"blk": dev}, device_id_type=pl.DeviceIdType.MESH,
        )

    def score_copy(src, dst, send_at, recv_at, dev):
        return pltpu.make_async_remote_copy(
            src_ref=ssend.at[src], dst_ref=ret.at[dst],
            send_sem=rs.at[send_at], recv_sem=rr.at[recv_at],
            device_id={"blk": dev}, device_id_type=pl.DeviceIdType.MESH,
        )

    pl.semaphore_wait(barrier, n - 1)

    def packed(chip):
        want = chip * PAIR + lax.broadcasted_iota(jnp.int32, (PAIR, rows), 0)
        pick = (slot == want).astype(jnp.float32).astype(jnp.bfloat16)
        moved = jnp.dot(pick, unit[...], preferred_element_type=jnp.float32)
        return moved.astype(jnp.bfloat16).reshape(2, SLOTS, emb.shape[1])

    def dispatch(j, _):
        off = nc // 2 + ((j + 1) // 2) * (1 - 2 * (j % 2))
        chip = (mine + off + nc) % nc
        send[pl.ds(2 * chip, 2)] = packed(chip)
        for h in range(2):
            d = 2 * chip + h
            unit_copy(d, me, d, me, d).start()
            key_copy(d, me, d, me, d).start()
        return 0

    lax.fori_loop(0, nc - 1, dispatch, 0)
    send[pl.ds(2 * mine, 2)] = packed(mine)
    unit_copy(mate, me, mate, me, mate).start()
    key_copy(mate, me, mate, me, mate).start()
    recv[me] = send[me]
    krecv[me] = ksend[me]

    def group_at(t):
        off = ((t + 1) // 2) * (2 * (t % 2) - 1)
        return (mine + off + nc) % nc

    def block(t_units, g):
        return jnp.exp2(
            dot_nt(t_units, recv[pl.ds(2 * g, 2)].reshape(PAIR, emb.shape[1])) * SHARPNESS
        )

    def key_rows(g):
        first, second = krecv[2 * g], krecv[2 * g + 1]
        both = jnp.concatenate([first, second], axis=1)
        return both[0:1], both[4:5]

    def fold(x):
        return x[:, :SLOTS] + x[:, SLOTS:]

    def step(t, _):
        g = group_at(t)
        for h in range(2):
            s = 2 * g + h

            @pl.when(s != me)
            def _():
                key_copy(s, s, s, s, s).wait_recv()
                unit_copy(s, s, s, s, s).wait_recv()

        krow, brow = key_rows(g)
        kc = jnp.transpose(jnp.broadcast_to(krow, (SLOTS, PAIR)))
        bc = jnp.transpose(jnp.broadcast_to(brow, (SLOTS, PAIR)))
        kc = jnp.concatenate([kc, kc], axis=1)
        bc = jnp.concatenate([bc, bc], axis=1)
        mine_units = recv[pl.ds(2 * g, 2)].reshape(PAIR, emb.shape[1])
        e = block(mine_units, g)
        acc = fold(jnp.where((bc == brow) & (krow < kc), e, 0.0))

        def against(u, acc):
            gu = group_at(u)
            kru, bru = key_rows(gu)
            e = jnp.where(bc == bru, block(mine_units, gu), 0.0)
            lower = jnp.where(kru < kc, e, 0.0)
            upper = (e - lower).reshape(PAIR // 8, 8, PAIR).sum(axis=0)
            rowacc[u] = rowacc[u] + upper
            return acc + fold(lower)

        acc = lax.fori_loop(0, t, against, acc)
        total = jnp.broadcast_to(jnp.sum(acc, axis=1, keepdims=True), (PAIR, SLOTS))
        as_row = jnp.transpose(total)[0:8, :]
        first = lax.broadcasted_iota(jnp.int32, (8, PAIR), 0) == 0
        rowacc[t] = jnp.where(first, as_row, 0.0)
        return 0

    lax.fori_loop(0, nc, step, 0)

    def give_back(t, _):
        g = group_at(t)
        scores = jnp.log1p(jnp.sum(rowacc[t], axis=0, keepdims=True))
        for h in range(2):
            s = 2 * g + h
            ssend[s] = jnp.broadcast_to(scores[:, h * SLOTS : (h + 1) * SLOTS], (8, SLOTS))

            @pl.when(s != me)
            def _():
                score_copy(s, me, s, me, s).start()

        return 0

    lax.fori_loop(0, nc, give_back, 0)
    ret[me] = ssend[me]

    def collect(k, _):
        s = (me + k) % n
        score_copy(s, s, s, s, s).wait_recv()
        return 0

    lax.fori_loop(1, n, collect, 0)

    back = ret[...][:, 0, :]
    hits_b = hits_f.astype(jnp.bfloat16)
    hi = back.astype(jnp.bfloat16)
    rest = back - hi.astype(jnp.float32)
    mid = rest.astype(jnp.bfloat16)
    low = (rest - mid.astype(jnp.float32)).astype(jnp.bfloat16)
    spread = sum(
        lax.dot_general(p, hits_b, (((0,), (0,)), ((), ())), preferred_element_type=jnp.float32)
        for p in (hi, mid, low)
    )
    out[...] = jnp.sum(jnp.where(at_slot, spread, 0.0), axis=0, keepdims=True)

    def drain(k, _):
        s = (me + k) % n
        unit_copy(s, s, s, s, s).wait_send()
        key_copy(s, s, s, s, s).wait_send()
        score_copy(s, s, s, s, s).wait_send()
        return 0

    lax.fori_loop(1, n, drain, 0)


def per_device(embeddings, owner_ids, local_cluster, arrival_rank):
    rows, width = embeddings.shape
    n = lax.axis_size("blk")
    nc = n // 2
    vmem = pl.BlockSpec(memory_space=pltpu.VMEM)
    dma = pltpu.SemaphoreType.DMA((n,))
    scores = pl.pallas_call(
        functools.partial(kernel, n),
        out_shape=jax.ShapeDtypeStruct((1, rows), jnp.float32),
        in_specs=[vmem] * 4,
        out_specs=vmem,
        scratch_shapes=[
            pltpu.VMEM((rows, width), jnp.bfloat16),
            pltpu.VMEM((n, SLOTS, width), jnp.bfloat16),
            pltpu.VMEM((n, SLOTS, width), jnp.bfloat16),
            pltpu.VMEM((n, 8, SLOTS), jnp.float32),
            pltpu.VMEM((n, 8, SLOTS), jnp.float32),
            pltpu.VMEM((nc, 8, PAIR), jnp.float32),
            pltpu.VMEM((n, 8, SLOTS), jnp.float32),
            pltpu.VMEM((n, 8, SLOTS), jnp.float32),
            dma, dma, dma, dma, dma, dma,
        ],
        compiler_params=pltpu.CompilerParams(
            collective_id=0, has_side_effects=True, vmem_limit_bytes=56 * 1024 * 1024
        ),
    )(
        embeddings,
        owner_ids.reshape(1, rows),
        local_cluster.reshape(1, rows),
        arrival_rank.reshape(1, rows),
    )
    return scores.reshape(rows)


def solution(mesh):
    return jax.shard_map(
        per_device,
        mesh=mesh,
        in_specs=(
            P(("parts", "blk"), None),
            P(("parts", "blk"), None),
            P(("parts", "blk")),
            P(("parts", "blk")),
        ),
        out_specs=P(("parts", "blk")),
        check_vma=False,
    )
```

```python
import functools

import jax
import jax.numpy as jnp
from jax import lax
from jax.experimental import pallas as pl
from jax.experimental.pallas import tpu as pltpu
from jax.sharding import PartitionSpec as P

CL_DEV = 64
LANES = 128
MESH = pl.DeviceIdType.MESH
SHARPNESS = 20.0 * 1.4426950408889634


def dot_nt(a, b):
    return lax.dot_general(a, b, (((1,), (1,)), ((), ())), preferred_element_type=jnp.float32)


def one_hot(ids, count):
    hits = ids == lax.broadcasted_iota(jnp.int32, (count, ids.shape[1]), 0)
    return hits, hits.astype(jnp.float32)


def narrow(x):
    return x.astype(jnp.bfloat16)


def below(count):
    first = lax.broadcasted_iota(jnp.int32, (count, count), 0)
    return first < lax.broadcasted_iota(jnp.int32, (count, count), 1)


def exact_dot(a, b):
    total = 0.0
    for _ in range(3):
        total = total + jnp.dot(narrow(a), b, preferred_element_type=jnp.float32)
        a = a - narrow(a).astype(jnp.float32)
    return total


def plan(n, groups, emb, own, lc, unit, tgt, most, cnt, tops, cs, cr, ts, tr):
    rows = emb.shape[0]
    me = lax.axis_index("blk")
    part = lax.axis_index("parts")

    barrier = pltpu.get_barrier_semaphore()

    def greet(k, _):
        pl.semaphore_signal(
            barrier, inc=1, device_id={"blk": (me + k) % n}, device_id_type=MESH
        )
        return 0

    lax.fori_loop(1, n, greet, 0)
    for k in range(1, groups):
        pl.semaphore_signal(
            barrier, inc=1, device_id={"parts": (part + k) % groups}, device_id_type=MESH
        )

    _, owner_f = one_hot(own[...], n)
    local, local_f = one_hot(lc[...], LANES)
    cnt[me] = dot_nt(narrow(owner_f), narrow(local_f))
    pl.semaphore_wait(barrier, n - 1 + groups - 1)

    def count_copy(src, dst, at, dev):
        return pltpu.make_async_remote_copy(
            src_ref=cnt.at[src], dst_ref=cnt.at[dst], send_sem=cs.at[at], recv_sem=cr.at[dst],
            device_id={"blk": dev}, device_id_type=MESH,
        )

    def send_counts(k, _):
        d = (me + k) % n
        count_copy(me, me, d, d).start()
        return 0

    lax.fori_loop(1, n, send_counts, 0)

    def normalise(i, _):
        span = pl.ds(pl.multiple_of(i * 128, 128), 128)
        wide = emb[span, :].astype(jnp.float32)
        inv = 1.0 / jnp.sqrt(jnp.sum(wide * wide, axis=1, keepdims=True) + 1e-06)
        unit[span, :] = narrow(wide * inv)
        return 0

    lax.fori_loop(0, rows // 128, normalise, 0)

    def take_counts(k, _):
        s = (me + k) % n
        count_copy(s, s, s, s).wait_recv()
        return 0

    lax.fori_loop(1, n, take_counts, 0)

    total = jnp.sum(cnt[...], axis=0)
    inside = exact_dot(total, narrow(below(LANES).astype(jnp.float32)))
    sums = jnp.broadcast_to(jnp.sum(total, axis=1, keepdims=True), (n, LANES))
    ahead = jnp.zeros((n, LANES), jnp.float32)
    line = lax.broadcasted_iota(jnp.int32, (n, LANES), 0)
    for o in range(n - 1):
        ahead = ahead + jnp.where(line > o, sums[o : o + 1], 0.0)
    middle = inside + ahead + 0.5 * total
    dest = jnp.minimum(jnp.floor(middle * (1.0 / rows)), float(n - 1))

    def widest(d, top):
        mask = (dest == d.astype(jnp.float32)).astype(jnp.float32)
        per_src = jnp.sum(cnt[...] * mask[None], axis=1)
        return jnp.maximum(top, jnp.sum(per_src, axis=1, keepdims=True))

    top = lax.fori_loop(0, n, widest, jnp.zeros((n, 1), jnp.float32))
    top = jnp.broadcast_to(jnp.max(top, axis=0, keepdims=True), (8, LANES))

    tops[part] = top

    def top_copy(src, dst, at, dev):
        return pltpu.make_async_remote_copy(
            src_ref=tops.at[src], dst_ref=tops.at[dst], send_sem=ts.at[at], recv_sem=tr.at[dst],
            device_id={"parts": dev}, device_id_type=MESH,
        )

    others = [(part + k) % groups for k in range(1, groups)]
    for d in others:
        top_copy(part, part, d, d).start()

    spread = lax.dot_general(
        narrow(dest), narrow(owner_f), (((0,), (0,)), ((), ())), preferred_element_type=jnp.float32
    )
    tgt[...] = jnp.sum(jnp.where(local, spread, 0.0), axis=0, keepdims=True).astype(jnp.int32)

    for d in others:
        top_copy(d, d, d, d).wait_recv()
    most[...] = jnp.max(tops[...], axis=0)
    for d in others:
        top_copy(d, d, d, d).wait_send()

    def drain(k, _):
        d = (me + k) % n
        count_copy(d, d, d, d).wait_send()
        return 0

    lax.fori_loop(1, n, drain, 0)


def kernel(
    n, SLOTS, q, unit, tgt, own, lc, rank, out,
    send, recv, ksend, krecv, krow, brow, rowacc, ssend, ret,
    us, ur, ks, kr, rs, rr,
):
    rows, width = unit.shape
    nc = n // 2
    ng = n // q
    PAIR = 2 * SLOTS
    span = q * SLOTS
    me = lax.axis_index("blk")
    mine = me // 2
    home = me // q
    mate = me + 1 - 2 * (me % 2)

    barrier = pltpu.get_barrier_semaphore()

    def greet(k, _):
        pl.semaphore_signal(
            barrier, inc=1, device_id={"blk": (me + k) % n}, device_id_type=MESH
        )
        return 0

    lax.fori_loop(1, n, greet, 0)

    target = tgt[...]
    _, hits_f = one_hot(target, n)
    earlier = jnp.dot(
        narrow(hits_f), narrow(below(rows).astype(jnp.float32)), preferred_element_type=jnp.float32
    )
    pos = jnp.sum(hits_f * earlier, axis=0, keepdims=True).astype(jnp.int32)
    slot = target * SLOTS + pos
    at_slot, at_slot_f = one_hot(pos, LANES)

    rank_v = rank[...]
    rank_hi = rank_v // 256
    rank_lo = rank_v - rank_hi * 256
    parts = [hits_f] + [
        hits_f * v.astype(jnp.float32) for v in (own[...], lc[...], rank_hi, rank_lo)
    ]
    table = [dot_nt(narrow(p), narrow(at_slot_f)) for p in parts]
    cluster = table[1] * float(CL_DEV) + table[2] + table[0] - 1.0
    order = table[3] * 256.0 + table[4]
    top = lax.broadcasted_iota(jnp.int32, (n, 8, LANES), 1) < 4
    ksend[...] = jnp.where(top, order[:, None, :], cluster[:, None, :])

    def key_copy(src, dst, send_at, recv_at, dev):
        return pltpu.make_async_remote_copy(
            src_ref=ksend.at[src], dst_ref=krecv.at[dst],
            send_sem=ks.at[send_at], recv_sem=kr.at[recv_at],
            device_id={"blk": dev}, device_id_type=MESH,
        )

    def unit_copy(src, dst, send_at, recv_at, dev):
        return pltpu.make_async_remote_copy(
            src_ref=send.at[src], dst_ref=recv.at[dst],
            send_sem=us.at[send_at], recv_sem=ur.at[recv_at],
            device_id={"blk": dev}, device_id_type=MESH,
        )

    def score_copy(src, dst, send_at, recv_at, dev):
        return pltpu.make_async_remote_copy(
            src_ref=ssend.at[src], dst_ref=ret.at[dst],
            send_sem=rs.at[send_at], recv_sem=rr.at[recv_at],
            device_id={"blk": dev}, device_id_type=MESH,
        )

    pl.semaphore_wait(barrier, n - 1)

    def packed(chip):
        want = chip * PAIR + lax.broadcasted_iota(jnp.int32, (PAIR, rows), 0)
        pick = (slot == want).astype(jnp.float32).astype(jnp.bfloat16)
        moved = jnp.dot(pick, unit[...], preferred_element_type=jnp.float32)
        return moved.astype(jnp.bfloat16).reshape(2, SLOTS, width)

    def dispatch(j, _):
        off = nc // 2 + ((j + 1) // 2) * (1 - 2 * (j % 2))
        chip = (mine + off + nc) % nc
        send[pl.ds(2 * chip, 2)] = packed(chip)
        for h in range(2):
            d = 2 * chip + h
            unit_copy(d, me, d, me, d).start()
            key_copy(d, me, d, me, d).start()
        return 0

    lax.fori_loop(0, nc - 1, dispatch, 0)
    send[pl.ds(2 * mine, 2)] = packed(mine)
    unit_copy(mate, me, mate, me, mate).start()
    key_copy(mate, me, mate, me, mate).start()
    recv[me] = send[me]
    krecv[me] = ksend[me]

    def group_at(t):
        off = ((t + 1) // 2) * (2 * (t % 2) - 1)
        return (home + off + ng) % ng

    def units_of(g):
        return recv[pl.ds(q * g, q)].reshape(span, width)

    def turned(line):
        return jnp.transpose(jnp.broadcast_to(line, (LANES, line.shape[1])))

    def fold(x):
        return sum(x[:, c : c + LANES] for c in range(0, span, LANES))

    def step(t, _):
        g = group_at(t)
        for h in range(q):
            s = q * g + h

            @pl.when(s != me)
            def _():
                key_copy(s, s, s, s, s).wait_recv()
                unit_copy(s, s, s, s, s).wait_recv()

        tiles = [krecv[q * g + h] for h in range(q)]
        kc = jnp.concatenate([turned(x[0:1])[0:SLOTS] for x in tiles], axis=0)
        bc = jnp.concatenate([turned(x[4:5])[0:SLOTS] for x in tiles], axis=0)
        krow[t] = jnp.transpose(kc)[0:8]
        brow[t] = jnp.transpose(bc)[0:8]
        kc = jnp.concatenate([kc] * (span // LANES), axis=1)
        bc = jnp.concatenate([bc] * (span // LANES), axis=1)
        here = units_of(g)

        def pairs(u, gu):
            e = jnp.exp2(dot_nt(here, units_of(gu)) * SHARPNESS)
            e = jnp.where(bc == brow[u][0:1], e, 0.0)
            return e, jnp.where(krow[u][0:1] < kc, e, 0.0)

        _, lower = pairs(t, g)
        acc = fold(lower)

        def against(u, acc):
            e, lower = pairs(u, group_at(u))
            rowacc[u] = rowacc[u] + (e - lower).reshape(span // 8, 8, span).sum(axis=0)
            return acc + fold(lower)

        acc = lax.fori_loop(0, t, against, acc)
        total = jnp.broadcast_to(jnp.sum(acc, axis=1, keepdims=True), (span, LANES))
        as_row = jnp.transpose(total)[0:8, :]
        first = lax.broadcasted_iota(jnp.int32, (8, span), 0) == 0
        rowacc[t] = jnp.where(first, as_row, 0.0)
        return 0

    lax.fori_loop(0, ng, step, 0)

    def give_back(t, _):
        g = group_at(t)
        scores = turned(jnp.log1p(jnp.sum(rowacc[t], axis=0, keepdims=True)))
        for h in range(q):
            s = q * g + h
            chunk = scores[h * SLOTS : (h + 1) * SLOTS]
            if SLOTS < LANES:
                empty = jnp.zeros((LANES - SLOTS, LANES), jnp.float32)
                chunk = jnp.concatenate([chunk, empty], axis=0)
            ssend[s] = jnp.transpose(chunk)[0:8]

            @pl.when(s != me)
            def _():
                score_copy(s, me, s, me, s).start()

        return 0

    lax.fori_loop(0, ng, give_back, 0)
    ret[me] = ssend[me]

    def collect(k, _):
        s = (me + k) % n
        score_copy(s, s, s, s, s).wait_recv()
        return 0

    lax.fori_loop(1, n, collect, 0)

    back = ret[...][:, 0, :]
    hits_b = hits_f.astype(jnp.bfloat16)
    hi = back.astype(jnp.bfloat16)
    rest = back - hi.astype(jnp.float32)
    mid = rest.astype(jnp.bfloat16)
    low = (rest - mid.astype(jnp.float32)).astype(jnp.bfloat16)
    spread = sum(
        lax.dot_general(p, hits_b, (((0,), (0,)), ((), ())), preferred_element_type=jnp.float32)
        for p in (hi, mid, low)
    )
    out[...] = jnp.sum(jnp.where(at_slot, spread, 0.0), axis=0, keepdims=True)

    def drain(k, _):
        s = (me + k) % n
        unit_copy(s, s, s, s, s).wait_send()
        key_copy(s, s, s, s, s).wait_send()
        score_copy(s, s, s, s, s).wait_send()
        return 0

    lax.fori_loop(1, n, drain, 0)


def params(number):
    return pltpu.CompilerParams(
        collective_id=number, has_side_effects=True, vmem_limit_bytes=56 * 1024 * 1024
    )


def exchange(number, n, slots, q, rows, width):
    ng = n // q
    vmem = pl.BlockSpec(memory_space=pltpu.VMEM)
    dma = pltpu.SemaphoreType.DMA((n,))
    return pl.pallas_call(
        functools.partial(kernel, n, slots, q),
        out_shape=jax.ShapeDtypeStruct((1, rows), jnp.float32),
        in_specs=[vmem] * 5,
        out_specs=vmem,
        scratch_shapes=[
            pltpu.VMEM((n, slots, width), jnp.bfloat16),
            pltpu.VMEM((n, slots, width), jnp.bfloat16),
            pltpu.VMEM((n, 8, LANES), jnp.float32),
            pltpu.VMEM((n, 8, LANES), jnp.float32),
            pltpu.VMEM((ng, 8, q * slots), jnp.float32),
            pltpu.VMEM((ng, 8, q * slots), jnp.float32),
            pltpu.VMEM((ng, 8, q * slots), jnp.float32),
            pltpu.VMEM((n, 8, LANES), jnp.float32),
            pltpu.VMEM((n, 8, LANES), jnp.float32),
            dma, dma, dma, dma, dma, dma,
        ],
        compiler_params=params(number),
    )


def per_device(embeddings, owner_ids, local_cluster, arrival_rank):
    rows, width = embeddings.shape
    n = lax.axis_size("blk")
    groups = lax.axis_size("parts")
    vmem = pl.BlockSpec(memory_space=pltpu.VMEM)
    small = -(-3 * rows // (2 * n) // 32) * 32
    owner = owner_ids.reshape(1, rows)
    local = local_cluster.reshape(1, rows)
    rank = arrival_rank.reshape(1, rows)
    unit, target, most = pl.pallas_call(
        functools.partial(plan, n, groups),
        out_shape=(
            jax.ShapeDtypeStruct((rows, width), jnp.bfloat16),
            jax.ShapeDtypeStruct((1, rows), jnp.int32),
            jax.ShapeDtypeStruct((8, LANES), jnp.float32),
        ),
        in_specs=[vmem] * 3,
        out_specs=(vmem,) * 3,
        scratch_shapes=[
            pltpu.VMEM((n, n, LANES), jnp.float32),
            pltpu.VMEM((groups, 8, LANES), jnp.float32),
            pltpu.SemaphoreType.DMA((n,)),
            pltpu.SemaphoreType.DMA((n,)),
            pltpu.SemaphoreType.DMA((groups,)),
            pltpu.SemaphoreType.DMA((groups,)),
        ],
        compiler_params=params(0),
    )(embeddings, owner, local)
    scores = lax.cond(
        most[0, 0] <= small,
        lambda: exchange(1, n, small, 4, rows, width)(unit, target, owner, local, rank),
        lambda: exchange(2, n, LANES, 2, rows, width)(unit, owner, owner, local, rank),
    )
    return scores.reshape(rows)


def solution(mesh):
    return jax.shard_map(
        per_device,
        mesh=mesh,
        in_specs=(
            P(("parts", "blk"), None),
            P(("parts", "blk"), None),
            P(("parts", "blk")),
            P(("parts", "blk")),
        ),
        out_specs=P(("parts", "blk")),
        check_vma=False,
    )
```

```python
import functools

import jax
import jax.numpy as jnp
from jax import lax
from jax.experimental import pallas as pl
from jax.experimental.pallas import tpu as pltpu
from jax.sharding import PartitionSpec as P

CL_DEV = 64
LANES = 128
MESH = pl.DeviceIdType.MESH
SHARPNESS = 20.0 * 1.4426950408889634


def dot_nt(a, b):
    return lax.dot_general(a, b, (((1,), (1,)), ((), ())), preferred_element_type=jnp.float32)


def one_hot(ids, count):
    hits = ids == lax.broadcasted_iota(jnp.int32, (count, ids.shape[1]), 0)
    return hits, hits.astype(jnp.float32)


def narrow(x):
    return x.astype(jnp.bfloat16)


def below(count):
    first = lax.broadcasted_iota(jnp.int32, (count, count), 0)
    return first < lax.broadcasted_iota(jnp.int32, (count, count), 1)


def exact_dot(a, b):
    total = 0.0
    for _ in range(3):
        total = total + jnp.dot(narrow(a), b, preferred_element_type=jnp.float32)
        a = a - narrow(a).astype(jnp.float32)
    return total


def plan(n, groups, near, far, emb, own, lc, unit, tgt, most, cnt, tops, cs, cr, ts, tr):
    rows = emb.shape[0]
    me = lax.axis_index("blk")
    part = lax.axis_index("parts")

    barrier = pltpu.get_barrier_semaphore()

    def greet(k, _):
        pl.semaphore_signal(
            barrier, inc=1, device_id={"blk": (me + k) % n}, device_id_type=MESH
        )
        return 0

    lax.fori_loop(1, n, greet, 0)
    for k in range(1, groups):
        pl.semaphore_signal(
            barrier, inc=1, device_id={"parts": (part + k) % groups}, device_id_type=MESH
        )

    _, owner_f = one_hot(own[...], n)
    local, local_f = one_hot(lc[...], LANES)
    cnt[me] = dot_nt(narrow(owner_f), narrow(local_f))
    pl.semaphore_wait(barrier, n - 1 + groups - 1)

    def count_copy(src, dst, at, dev):
        return pltpu.make_async_remote_copy(
            src_ref=cnt.at[src], dst_ref=cnt.at[dst], send_sem=cs.at[at], recv_sem=cr.at[dst],
            device_id={"blk": dev}, device_id_type=MESH,
        )

    def send_counts(k, _):
        d = (me + k) % n
        count_copy(me, me, d, d).start()
        return 0

    lax.fori_loop(1, n, send_counts, 0)

    def normalise(i, _):
        span = pl.ds(pl.multiple_of(i * 128, 128), 128)
        wide = emb[span, :].astype(jnp.float32)
        inv = 1.0 / jnp.sqrt(jnp.sum(wide * wide, axis=1, keepdims=True) + 1e-06)
        unit[span, :] = narrow(wide * inv)
        return 0

    lax.fori_loop(0, rows // 128, normalise, 0)

    def take_counts(k, _):
        s = (me + k) % n
        count_copy(s, s, s, s).wait_recv()
        return 0

    lax.fori_loop(1, n, take_counts, 0)

    half = n // 2
    total = jnp.sum(cnt[...], axis=0)
    lean = total - 2.0 * jnp.sum(cnt[0:half], axis=0)
    line = lax.broadcasted_iota(jnp.int32, (n, LANES), 0)
    number = line * CL_DEV + lax.broadcasted_iota(jnp.int32, (n, LANES), 1)
    lean = lean + ((number * 7) % 16).astype(jnp.float32) * 0.0625

    def whole(x):
        return jnp.sum(jnp.sum(x, axis=0, keepdims=True), axis=1, keepdims=True)

    edge = jnp.full((1, 1), -4.0, jnp.float32)
    for move in (4.0, 2.0, 1.0, 0.5, 0.25, 0.125, 0.0625):
        upper = whole(jnp.where(lean > edge + move, total, 0.0))
        edge = jnp.where(upper > 0.5 * n * rows, edge + move, edge)
    high = lean > edge
    dest = jnp.zeros((n, LANES), jnp.float32)
    for chosen, start in ((high, half), (jnp.logical_not(high), 0)):
        mass = jnp.where(chosen, total, 0.0)
        inside = exact_dot(mass, narrow(below(LANES).astype(jnp.float32)))
        sums = jnp.broadcast_to(jnp.sum(mass, axis=1, keepdims=True), (n, LANES))
        ahead = jnp.zeros((n, LANES), jnp.float32)
        for o in range(n - 1):
            ahead = ahead + jnp.where(line > o, sums[o : o + 1], 0.0)
        scale = half / jnp.maximum(whole(mass), 1.0)
        index = jnp.floor((inside + ahead + 0.5 * mass) * scale)
        dest = jnp.where(chosen, jnp.minimum(index, half - 1.0) + float(start), dest)

    source = lax.broadcasted_iota(jnp.int32, (n, 1), 0) // half

    def widest(d, top):
        mask = (dest == d.astype(jnp.float32)).astype(jnp.float32)
        per_src = jnp.sum(jnp.sum(cnt[...] * mask[None], axis=1), axis=1, keepdims=True)
        room = jnp.where(source == d // half, float(near), float(far))
        return jnp.maximum(top, per_src - room)

    top = lax.fori_loop(0, n, widest, jnp.full((n, 1), -float(rows), jnp.float32))
    top = jnp.broadcast_to(jnp.max(top, axis=0, keepdims=True), (8, LANES))

    tops[part] = top

    def top_copy(src, dst, at, dev):
        return pltpu.make_async_remote_copy(
            src_ref=tops.at[src], dst_ref=tops.at[dst], send_sem=ts.at[at], recv_sem=tr.at[dst],
            device_id={"parts": dev}, device_id_type=MESH,
        )

    others = [(part + k) % groups for k in range(1, groups)]
    for d in others:
        top_copy(part, part, d, d).start()

    spread = lax.dot_general(
        narrow(dest), narrow(owner_f), (((0,), (0,)), ((), ())), preferred_element_type=jnp.float32
    )
    tgt[...] = jnp.sum(jnp.where(local, spread, 0.0), axis=0, keepdims=True).astype(jnp.int32)

    for d in others:
        top_copy(d, d, d, d).wait_recv()
    most[...] = jnp.max(tops[...], axis=0)
    for d in others:
        top_copy(d, d, d, d).wait_send()

    def drain(k, _):
        d = (me + k) % n
        count_copy(d, d, d, d).wait_send()
        return 0

    lax.fori_loop(1, n, drain, 0)


def kernel(
    n, near, far, tile, unit, tgt, own, lc, rank, out,
    send, recv_near, recv_far, ksend, krecv, kc_near, bc_near, kc_far, bc_far,
    acc_near, col_far, ssend, ret,
    us, ur, ks, kr, rs, rr,
):
    rows, width = unit.shape
    nc = n // 2
    half = n // 2
    hc = half // 2
    me = lax.axis_index("blk")
    here = me % half
    mine = here // 2
    base_near = me - here
    base_far = half - base_near
    mate = me + 1 - 2 * (me % 2)

    barrier = pltpu.get_barrier_semaphore()

    def greet(k, _):
        pl.semaphore_signal(
            barrier, inc=1, device_id={"blk": (me + k) % n}, device_id_type=MESH
        )
        return 0

    lax.fori_loop(1, n, greet, 0)

    target = tgt[...]
    _, hits_f = one_hot(target, n)
    earlier = jnp.dot(
        narrow(hits_f), narrow(below(rows).astype(jnp.float32)), preferred_element_type=jnp.float32
    )
    pos = jnp.sum(hits_f * earlier, axis=0, keepdims=True).astype(jnp.int32)
    slot = target * LANES + pos
    at_slot, at_slot_f = one_hot(pos, LANES)

    rank_v = rank[...]
    rank_hi = rank_v // 256
    rank_lo = rank_v - rank_hi * 256
    parts = [hits_f] + [
        hits_f * v.astype(jnp.float32) for v in (own[...], lc[...], rank_hi, rank_lo)
    ]
    table = [dot_nt(narrow(p), narrow(at_slot_f)) for p in parts]
    cluster = table[1] * float(CL_DEV) + table[2] + table[0] - 1.0
    order = table[3] * 256.0 + table[4]
    top = lax.broadcasted_iota(jnp.int32, (n, 8, LANES), 1) < 4
    ksend[...] = jnp.where(top, order[:, None, :], cluster[:, None, :])

    def key_copy(src, dst, send_at, recv_at, dev):
        return pltpu.make_async_remote_copy(
            src_ref=ksend.at[src], dst_ref=krecv.at[dst],
            send_sem=ks.at[send_at], recv_sem=kr.at[recv_at],
            device_id={"blk": dev}, device_id_type=MESH,
        )

    def unit_copy(src, dst, send_at, recv_at, dev, close):
        room = near if close else far
        into = recv_near if close else recv_far
        return pltpu.make_async_remote_copy(
            src_ref=send.at[src, pl.ds(0, room)], dst_ref=into.at[dst],
            send_sem=us.at[send_at], recv_sem=ur.at[recv_at],
            device_id={"blk": dev}, device_id_type=MESH,
        )

    def score_copy(src, dst, send_at, recv_at, dev):
        return pltpu.make_async_remote_copy(
            src_ref=ssend.at[src], dst_ref=ret.at[dst],
            send_sem=rs.at[send_at], recv_sem=rr.at[recv_at],
            device_id={"blk": dev}, device_id_type=MESH,
        )

    pl.semaphore_wait(barrier, n - 1)

    def send_keys(k, _):
        d = (me + k) % n
        key_copy(d, me, d, me, d).start()
        return 0

    lax.fori_loop(1, n, send_keys, 0)

    def pack(first):
        want = first * LANES + lax.broadcasted_iota(jnp.int32, (2 * LANES, rows), 0)
        pick = narrow((slot == want).astype(jnp.float32))
        moved = jnp.dot(pick, unit[...], preferred_element_type=jnp.float32)
        send[pl.ds(first, 2)] = narrow(moved).reshape(2, LANES, width)

    def dispatch_far(j, _):
        first = base_far + 2 * ((mine + j) % hc)
        pack(first)
        for h in range(2):
            unit_copy(first + h, here, first + h, me, first + h, False).start()
        return 0

    def dispatch_near(j, _):
        first = base_near + 2 * ((mine + j) % hc)
        pack(first)
        for h in range(2):
            unit_copy(first + h, here, first + h, me, first + h, True).start()
        return 0

    lax.fori_loop(0, hc, dispatch_far, 0)
    lax.fori_loop(1, hc, dispatch_near, 0)
    pack(base_near + 2 * mine)
    unit_copy(mate, here, mate, me, mate, True).start()
    recv_near[here] = send[me, 0:near]
    krecv[me] = ksend[me]

    def take_keys(k, _):
        s = (me + k) % n
        key_copy(s, s, s, s, s).wait_recv()
        return 0

    lax.fori_loop(1, n, take_keys, 0)

    def turned(line):
        return jnp.transpose(jnp.broadcast_to(line, (LANES, line.shape[1])))

    def keys(base, room, kc, bc):
        for h in range(half):
            x = krecv[base + h]
            kc[h * room : (h + 1) * room] = turned(x[0:1])[0:room]
            bc[h * room : (h + 1) * room] = turned(x[4:5])[0:room]
        return jnp.transpose(kc[...])[0:1], jnp.transpose(bc[...])[0:1]

    kr_near, br_near = keys(base_near, near, kc_near, bc_near)
    kr_far, br_far = keys(base_far, far, kc_far, bc_far)

    def wide(x, lanes):
        return jnp.concatenate([x] * (lanes // LANES), axis=1)

    def fold(x):
        return sum(x[:, c : c + LANES] for c in range(0, x.shape[1], LANES))

    def down(x):
        return x.reshape(x.shape[0] // 8, 8, x.shape[1]).sum(axis=0)

    def pairs(recv, p, room, kc, bc, other, kr, br):
        lanes = other.shape[0] * other.shape[1]
        left = recv[pl.ds(tile * p, tile)].reshape(tile * room, width)
        at = pl.ds(pl.multiple_of(p * (tile * room), 16), tile * room)
        e = jnp.exp2(dot_nt(left, other[...].reshape(lanes, width)) * SHARPNESS)
        e = jnp.where(wide(bc[at], lanes) == br, e, 0.0)
        return at, e, wide(kc[at], lanes) < kr

    def wait_near(k, _):
        s = (here + k) % half
        d = base_near + s
        unit_copy(d, s, d, d, d, True).wait_recv()
        return 0

    lax.fori_loop(1, half, wait_near, 0)

    def near_near(p, acc):
        _, e, before = pairs(recv_near, p, near, kc_near, bc_near, recv_near, kr_near, br_near)
        return acc + down(jnp.where(before, e, 0.0))

    acc_near[...] = lax.fori_loop(
        0, half // tile, near_near, jnp.zeros((8, half * near), jnp.float32)
    )

    def far_near(j, _):
        p = (here // tile - j + half // tile) % (half // tile)
        for h in range(tile):
            s = tile * p + h
            d = base_far + s
            unit_copy(d, s, d, d, d, False).wait_recv()
        at, e, before = pairs(recv_far, p, far, kc_far, bc_far, recv_near, kr_near, br_near)
        lower = jnp.where(before, e, 0.0)
        acc_near[...] = acc_near[...] + down(lower)
        sums = jnp.sum(fold(e - lower), axis=1, keepdims=True)
        col_far[at] = jnp.broadcast_to(sums, (tile * far, LANES))
        return 0

    lax.fori_loop(0, half // tile, far_near, 0)

    def give_back(h, base, column):
        s = base + h
        room = column.shape[0]
        if room < LANES:
            empty = jnp.zeros((LANES - room, LANES), jnp.float32)
            column = jnp.concatenate([column, empty], axis=0)
        ssend[s] = jnp.transpose(column)[0:8]

        @pl.when(s != me)
        def _():
            score_copy(s, me, s, me, s).start()

    scores = turned(jnp.log1p(jnp.sum(acc_near[...], axis=0, keepdims=True)))
    for h in range(half):
        give_back(h, base_near, scores[h * near : (h + 1) * near])

    def far_far(p, acc):
        _, e, before = pairs(recv_far, p, far, kc_far, bc_far, recv_far, kr_far, br_far)
        return acc + down(jnp.where(before, e, 0.0))

    acc = lax.fori_loop(0, half // tile, far_far, jnp.zeros((8, half * far), jnp.float32))
    scores = jnp.log1p(turned(jnp.sum(acc, axis=0, keepdims=True)) + col_far[...])
    for h in range(half):
        give_back(h, base_far, scores[h * far : (h + 1) * far])
    ret[me] = ssend[me]

    def collect(k, _):
        s = (me + k) % n
        score_copy(s, s, s, s, s).wait_recv()
        return 0

    lax.fori_loop(1, n, collect, 0)

    back = ret[...][:, 0, :]
    hits_b = hits_f.astype(jnp.bfloat16)
    hi = back.astype(jnp.bfloat16)
    rest = back - hi.astype(jnp.float32)
    mid = rest.astype(jnp.bfloat16)
    low = (rest - mid.astype(jnp.float32)).astype(jnp.bfloat16)
    spread = sum(
        lax.dot_general(p, hits_b, (((0,), (0,)), ((), ())), preferred_element_type=jnp.float32)
        for p in (hi, mid, low)
    )
    out[...] = jnp.sum(jnp.where(at_slot, spread, 0.0), axis=0, keepdims=True)

    def drain(k, _):
        s = (me + k) % n
        key_copy(s, s, s, s, s).wait_send()
        score_copy(s, s, s, s, s).wait_send()
        return 0

    def drain_near(k, _):
        s = (here + k) % half
        d = base_near + s
        unit_copy(d, s, d, d, d, True).wait_send()
        return 0

    def drain_far(s, _):
        d = base_far + s
        unit_copy(d, s, d, d, d, False).wait_send()
        return 0

    lax.fori_loop(1, n, drain, 0)
    lax.fori_loop(1, half, drain_near, 0)
    lax.fori_loop(0, half, drain_far, 0)


def params(number):
    return pltpu.CompilerParams(
        collective_id=number, has_side_effects=True, vmem_limit_bytes=56 * 1024 * 1024
    )


def exchange(number, n, near, far, rows, width):
    half = n // 2
    tile = 2 if half * near <= 1024 else 1
    vmem = pl.BlockSpec(memory_space=pltpu.VMEM)
    dma = pltpu.SemaphoreType.DMA((n,))
    return pl.pallas_call(
        functools.partial(kernel, n, near, far, tile),
        out_shape=jax.ShapeDtypeStruct((1, rows), jnp.float32),
        in_specs=[vmem] * 5,
        out_specs=vmem,
        scratch_shapes=[
            pltpu.VMEM((n, LANES, width), jnp.bfloat16),
            pltpu.VMEM((half, near, width), jnp.bfloat16),
            pltpu.VMEM((half, far, width), jnp.bfloat16),
            pltpu.VMEM((n, 8, LANES), jnp.float32),
            pltpu.VMEM((n, 8, LANES), jnp.float32),
            pltpu.VMEM((half * near, LANES), jnp.float32),
            pltpu.VMEM((half * near, LANES), jnp.float32),
            pltpu.VMEM((half * far, LANES), jnp.float32),
            pltpu.VMEM((half * far, LANES), jnp.float32),
            pltpu.VMEM((8, half * near), jnp.float32),
            pltpu.VMEM((half * far, LANES), jnp.float32),
            pltpu.VMEM((n, 8, LANES), jnp.float32),
            pltpu.VMEM((n, 8, LANES), jnp.float32),
            dma, dma, dma, dma, dma, dma,
        ],
        compiler_params=params(number),
    )


def per_device(embeddings, owner_ids, local_cluster, arrival_rank):
    rows, width = embeddings.shape
    n = lax.axis_size("blk")
    groups = lax.axis_size("parts")
    vmem = pl.BlockSpec(memory_space=pltpu.VMEM)
    near = min(LANES, -(-7 * rows // (4 * n) // 16) * 16)
    far = min(LANES, -(-5 * rows // (4 * n) // 16) * 16)
    owner = owner_ids.reshape(1, rows)
    local = local_cluster.reshape(1, rows)
    rank = arrival_rank.reshape(1, rows)
    unit, target, most = pl.pallas_call(
        functools.partial(plan, n, groups, near, far),
        out_shape=(
            jax.ShapeDtypeStruct((rows, width), jnp.bfloat16),
            jax.ShapeDtypeStruct((1, rows), jnp.int32),
            jax.ShapeDtypeStruct((8, LANES), jnp.float32),
        ),
        in_specs=[vmem] * 3,
        out_specs=(vmem,) * 3,
        scratch_shapes=[
            pltpu.VMEM((n, n, LANES), jnp.float32),
            pltpu.VMEM((groups, 8, LANES), jnp.float32),
            pltpu.SemaphoreType.DMA((n,)),
            pltpu.SemaphoreType.DMA((n,)),
            pltpu.SemaphoreType.DMA((groups,)),
            pltpu.SemaphoreType.DMA((groups,)),
        ],
        compiler_params=params(0),
    )(embeddings, owner, local)
    scores = lax.cond(
        most[0, 0] <= 0.0,
        lambda: exchange(1, n, near, far, rows, width)(unit, target, owner, local, rank),
        lambda: exchange(2, n, LANES, LANES, rows, width)(unit, owner, owner, local, rank),
    )
    return scores.reshape(rows)


def solution(mesh):
    return jax.shard_map(
        per_device,
        mesh=mesh,
        in_specs=(
            P(("parts", "blk"), None),
            P(("parts", "blk"), None),
            P(("parts", "blk")),
            P(("parts", "blk")),
        ),
        out_specs=P(("parts", "blk")),
        check_vma=False,
    )
```

```python
import functools

import jax
import jax.numpy as jnp
from jax import lax
from jax.experimental import pallas as pl
from jax.experimental.pallas import tpu as pltpu
from jax.sharding import PartitionSpec as P

CL_DEV = 64
LANES = 128
MESH = pl.DeviceIdType.MESH
SHARPNESS = 20.0 * 1.4426950408889634


def dot_nt(a, b):
    return lax.dot_general(a, b, (((1,), (1,)), ((), ())), preferred_element_type=jnp.float32)


def one_hot(ids, count):
    hits = ids == lax.broadcasted_iota(jnp.int32, (count, ids.shape[1]), 0)
    return hits, hits.astype(jnp.float32)


def narrow(x):
    return x.astype(jnp.bfloat16)


def below(count):
    first = lax.broadcasted_iota(jnp.int32, (count, count), 0)
    return first < lax.broadcasted_iota(jnp.int32, (count, count), 1)


def exact_dot(a, b):
    total = 0.0
    for _ in range(3):
        total = total + jnp.dot(narrow(a), b, preferred_element_type=jnp.float32)
        a = a - narrow(a).astype(jnp.float32)
    return total


def plan(n, groups, near, far, emb, own, lc, unit, tgt, most, cnt, tops, cs, cr, ts, tr):
    rows = emb.shape[0]
    me = lax.axis_index("blk")
    part = lax.axis_index("parts")

    barrier = pltpu.get_barrier_semaphore()

    def greet(k, _):
        pl.semaphore_signal(
            barrier, inc=1, device_id={"blk": (me + k) % n}, device_id_type=MESH
        )
        return 0

    lax.fori_loop(1, n, greet, 0)
    for k in range(1, groups):
        pl.semaphore_signal(
            barrier, inc=1, device_id={"parts": (part + k) % groups}, device_id_type=MESH
        )

    _, owner_f = one_hot(own[...], n)
    local, local_f = one_hot(lc[...], LANES)
    cnt[me] = dot_nt(narrow(owner_f), narrow(local_f))
    pl.semaphore_wait(barrier, n - 1 + groups - 1)

    def count_copy(src, dst, at, dev):
        return pltpu.make_async_remote_copy(
            src_ref=cnt.at[src], dst_ref=cnt.at[dst], send_sem=cs.at[at], recv_sem=cr.at[dst],
            device_id={"blk": dev}, device_id_type=MESH,
        )

    def send_counts(k, _):
        d = (me + k) % n
        count_copy(me, me, d, d).start()
        return 0

    lax.fori_loop(1, n, send_counts, 0)

    def normalise(i, _):
        span = pl.ds(pl.multiple_of(i * 128, 128), 128)
        wide = emb[span, :].astype(jnp.float32)
        inv = 1.0 / jnp.sqrt(jnp.sum(wide * wide, axis=1, keepdims=True) + 1e-06)
        unit[span, :] = narrow(wide * inv)
        return 0

    lax.fori_loop(0, rows // 128, normalise, 0)

    def take_counts(k, _):
        s = (me + k) % n
        count_copy(s, s, s, s).wait_recv()
        return 0

    lax.fori_loop(1, n, take_counts, 0)

    half = n // 2
    total = jnp.sum(cnt[...], axis=0)
    lean = total - 2.0 * jnp.sum(cnt[0:half], axis=0)
    line = lax.broadcasted_iota(jnp.int32, (n, LANES), 0)
    number = line * CL_DEV + lax.broadcasted_iota(jnp.int32, (n, LANES), 1)
    lean = lean + ((number * 7) % 16).astype(jnp.float32) * 0.0625

    def whole(x):
        return jnp.sum(jnp.sum(x, axis=0, keepdims=True), axis=1, keepdims=True)

    edge = jnp.full((1, 1), -4.0, jnp.float32)
    for move in (4.0, 2.0, 1.0, 0.5, 0.25, 0.125, 0.0625):
        upper = whole(jnp.where(lean > edge + move, total, 0.0))
        edge = jnp.where(upper > 0.5 * n * rows, edge + move, edge)
    high = lean > edge
    dest = jnp.zeros((n, LANES), jnp.float32)
    for chosen, start in ((high, half), (jnp.logical_not(high), 0)):
        mass = jnp.where(chosen, total, 0.0)
        inside = exact_dot(mass, narrow(below(LANES).astype(jnp.float32)))
        sums = jnp.broadcast_to(jnp.sum(mass, axis=1, keepdims=True), (n, LANES))
        ahead = jnp.zeros((n, LANES), jnp.float32)
        for o in range(n - 1):
            ahead = ahead + jnp.where(line > o, sums[o : o + 1], 0.0)
        scale = half / jnp.maximum(whole(mass), 1.0)
        index = jnp.floor((inside + ahead + 0.5 * mass) * scale)
        dest = jnp.where(chosen, jnp.minimum(index, half - 1.0) + float(start), dest)

    by_owner = jnp.transpose(cnt[...], (1, 0, 2))
    device = lax.broadcasted_iota(jnp.int32, (n, LANES), 0).astype(jnp.float32)
    load = jnp.zeros((n, n), jnp.float32)
    for o in range(n):
        mask = (dest[o : o + 1] == device).astype(jnp.float32)
        load = load + dot_nt(narrow(by_owner[o]), narrow(mask))
    source = lax.broadcasted_iota(jnp.int32, (n, n), 0) // half
    place = lax.broadcasted_iota(jnp.int32, (n, n), 1) // half
    over = load - jnp.where(source == place, float(near), float(far))
    top = jnp.max(jnp.max(over, axis=0, keepdims=True), axis=1, keepdims=True)
    top = jnp.broadcast_to(top, (8, LANES))

    tops[part] = top

    def top_copy(src, dst, at, dev):
        return pltpu.make_async_remote_copy(
            src_ref=tops.at[src], dst_ref=tops.at[dst], send_sem=ts.at[at], recv_sem=tr.at[dst],
            device_id={"parts": dev}, device_id_type=MESH,
        )

    others = [(part + k) % groups for k in range(1, groups)]
    for d in others:
        top_copy(part, part, d, d).start()

    spread = lax.dot_general(
        narrow(dest), narrow(owner_f), (((0,), (0,)), ((), ())), preferred_element_type=jnp.float32
    )
    tgt[...] = jnp.sum(jnp.where(local, spread, 0.0), axis=0, keepdims=True).astype(jnp.int32)

    for d in others:
        top_copy(d, d, d, d).wait_recv()
    most[0, 0] = jnp.max(tops[...])
    for d in others:
        top_copy(d, d, d, d).wait_send()

    def drain(k, _):
        d = (me + k) % n
        count_copy(d, d, d, d).wait_send()
        return 0

    lax.fori_loop(1, n, drain, 0)


def kernel(
    n, near, far, tile, unit, tgt, own, lc, rank, out,
    send, recv_near, recv_far, ksend, krecv, kc_near, bc_near, kc_far, bc_far,
    acc_near, col_far, ssend, ret,
    us, ur, ks, kr, rs, rr,
):
    rows, width = unit.shape
    nc = n // 2
    half = n // 2
    hc = half // 2
    me = lax.axis_index("blk")
    here = me % half
    mine = here // 2
    base_near = me - here
    base_far = half - base_near
    mate = me + 1 - 2 * (me % 2)

    barrier = pltpu.get_barrier_semaphore()

    def greet(k, _):
        pl.semaphore_signal(
            barrier, inc=1, device_id={"blk": (me + k) % n}, device_id_type=MESH
        )
        return 0

    lax.fori_loop(1, n, greet, 0)

    target = tgt[...]
    _, hits_f = one_hot(target, n)
    earlier = jnp.dot(
        narrow(hits_f), narrow(below(rows).astype(jnp.float32)), preferred_element_type=jnp.float32
    )
    pos = jnp.sum(hits_f * earlier, axis=0, keepdims=True).astype(jnp.int32)
    slot = target * LANES + pos
    at_slot, at_slot_f = one_hot(pos, LANES)

    rank_v = rank[...]
    rank_hi = rank_v // 256
    rank_lo = rank_v - rank_hi * 256
    parts = [hits_f] + [
        hits_f * v.astype(jnp.float32) for v in (own[...], lc[...], rank_hi, rank_lo)
    ]
    table = [dot_nt(narrow(p), narrow(at_slot_f)) for p in parts]
    cluster = table[1] * float(CL_DEV) + table[2] + table[0] - 1.0
    order = table[3] * 256.0 + table[4]
    top = lax.broadcasted_iota(jnp.int32, (n, 8, LANES), 1) < 4
    ksend[...] = jnp.where(top, order[:, None, :], cluster[:, None, :])

    def key_copy(src, dst, send_at, recv_at, dev):
        return pltpu.make_async_remote_copy(
            src_ref=ksend.at[src], dst_ref=krecv.at[dst],
            send_sem=ks.at[send_at], recv_sem=kr.at[recv_at],
            device_id={"blk": dev}, device_id_type=MESH,
        )

    def unit_copy(src, dst, send_at, recv_at, dev, close):
        room = near if close else far
        into = recv_near if close else recv_far
        return pltpu.make_async_remote_copy(
            src_ref=send.at[src, pl.ds(0, room)], dst_ref=into.at[dst],
            send_sem=us.at[send_at], recv_sem=ur.at[recv_at],
            device_id={"blk": dev}, device_id_type=MESH,
        )

    def score_copy(src, dst, send_at, recv_at, dev):
        return pltpu.make_async_remote_copy(
            src_ref=ssend.at[src], dst_ref=ret.at[dst],
            send_sem=rs.at[send_at], recv_sem=rr.at[recv_at],
            device_id={"blk": dev}, device_id_type=MESH,
        )

    pl.semaphore_wait(barrier, n - 1)

    def send_keys(k, _):
        d = (me + k) % n
        key_copy(d, me, d, me, d).start()
        return 0

    lax.fori_loop(1, n, send_keys, 0)

    def pack(first):
        want = first * LANES + lax.broadcasted_iota(jnp.int32, (2 * LANES, rows), 0)
        pick = narrow((slot == want).astype(jnp.float32))
        moved = jnp.dot(pick, unit[...], preferred_element_type=jnp.float32)
        send[pl.ds(first, 2)] = narrow(moved).reshape(2, LANES, width)

    def dispatch_far(j, _):
        first = base_far + 2 * ((mine + j) % hc)
        pack(first)
        for h in range(2):
            unit_copy(first + h, here, first + h, me, first + h, False).start()
        return 0

    def dispatch_near(j, _):
        first = base_near + 2 * ((mine + j) % hc)
        pack(first)
        for h in range(2):
            unit_copy(first + h, here, first + h, me, first + h, True).start()
        return 0

    lax.fori_loop(0, hc, dispatch_far, 0)
    lax.fori_loop(1, hc, dispatch_near, 0)
    pack(base_near + 2 * mine)
    unit_copy(mate, here, mate, me, mate, True).start()
    recv_near[here] = send[me, 0:near]
    krecv[me] = ksend[me]

    def take_keys(k, _):
        s = (me + k) % n
        key_copy(s, s, s, s, s).wait_recv()
        return 0

    lax.fori_loop(1, n, take_keys, 0)

    def turned(line):
        return jnp.transpose(jnp.broadcast_to(line, (LANES, line.shape[1])))

    def keys(base, room, kc, bc):
        for h in range(half):
            x = krecv[base + h]
            kc[h * room : (h + 1) * room] = turned(x[0:1])[0:room]
            bc[h * room : (h + 1) * room] = turned(x[4:5])[0:room]
        return jnp.transpose(kc[...])[0:1], jnp.transpose(bc[...])[0:1]

    kr_near, br_near = keys(base_near, near, kc_near, bc_near)
    kr_far, br_far = keys(base_far, far, kc_far, bc_far)

    def wide(x, lanes):
        return jnp.concatenate([x] * (lanes // LANES), axis=1)

    def fold(x):
        return sum(x[:, c : c + LANES] for c in range(0, x.shape[1], LANES))

    def down(x):
        return x.reshape(x.shape[0] // 8, 8, x.shape[1]).sum(axis=0)

    def pairs(recv, p, room, kc, bc, other, kr, br):
        lanes = other.shape[0] * other.shape[1]
        left = recv[pl.ds(tile * p, tile)].reshape(tile * room, width)
        at = pl.ds(pl.multiple_of(p * (tile * room), 16), tile * room)
        e = jnp.exp2(dot_nt(left, other[...].reshape(lanes, width)) * SHARPNESS)
        e = jnp.where(wide(bc[at], lanes) == br, e, 0.0)
        return at, e, wide(kc[at], lanes) < kr

    def wait_near(k, _):
        s = (here + k) % half
        d = base_near + s
        unit_copy(d, s, d, d, d, True).wait_recv()
        return 0

    lax.fori_loop(1, half, wait_near, 0)

    def near_near(p, acc):
        _, e, before = pairs(recv_near, p, near, kc_near, bc_near, recv_near, kr_near, br_near)
        return acc + down(jnp.where(before, e, 0.0))

    acc_near[...] = lax.fori_loop(
        0, half // tile, near_near, jnp.zeros((8, half * near), jnp.float32)
    )

    def far_near(j, _):
        p = (here // tile - j + half // tile) % (half // tile)
        for h in range(tile):
            s = tile * p + h
            d = base_far + s
            unit_copy(d, s, d, d, d, False).wait_recv()
        at, e, before = pairs(recv_far, p, far, kc_far, bc_far, recv_near, kr_near, br_near)
        lower = jnp.where(before, e, 0.0)
        acc_near[...] = acc_near[...] + down(lower)
        sums = jnp.sum(fold(e - lower), axis=1, keepdims=True)
        col_far[at] = jnp.broadcast_to(sums, (tile * far, LANES))
        return 0

    lax.fori_loop(0, half // tile, far_near, 0)

    def give_back(h, base, column):
        s = base + h
        room = column.shape[0]
        if room < LANES:
            empty = jnp.zeros((LANES - room, LANES), jnp.float32)
            column = jnp.concatenate([column, empty], axis=0)
        ssend[s] = jnp.transpose(column)[0:8]

        @pl.when(s != me)
        def _():
            score_copy(s, me, s, me, s).start()

    scores = turned(jnp.log1p(jnp.sum(acc_near[...], axis=0, keepdims=True)))
    for h in range(half):
        give_back(h, base_near, scores[h * near : (h + 1) * near])

    def far_far(p, acc):
        _, e, before = pairs(recv_far, p, far, kc_far, bc_far, recv_far, kr_far, br_far)
        return acc + down(jnp.where(before, e, 0.0))

    acc = lax.fori_loop(0, half // tile, far_far, jnp.zeros((8, half * far), jnp.float32))
    scores = jnp.log1p(turned(jnp.sum(acc, axis=0, keepdims=True)) + col_far[...])
    for h in range(half):
        give_back(h, base_far, scores[h * far : (h + 1) * far])
    ret[me] = ssend[me]

    def collect(k, _):
        s = (me + k) % n
        score_copy(s, s, s, s, s).wait_recv()
        return 0

    lax.fori_loop(1, n, collect, 0)

    back = ret[...][:, 0, :]
    hits_b = hits_f.astype(jnp.bfloat16)
    hi = back.astype(jnp.bfloat16)
    rest = back - hi.astype(jnp.float32)
    mid = rest.astype(jnp.bfloat16)
    low = (rest - mid.astype(jnp.float32)).astype(jnp.bfloat16)
    spread = sum(
        lax.dot_general(p, hits_b, (((0,), (0,)), ((), ())), preferred_element_type=jnp.float32)
        for p in (hi, mid, low)
    )
    out[...] = jnp.sum(jnp.where(at_slot, spread, 0.0), axis=0, keepdims=True)

    def drain(k, _):
        s = (me + k) % n
        key_copy(s, s, s, s, s).wait_send()
        score_copy(s, s, s, s, s).wait_send()
        return 0

    def drain_near(k, _):
        s = (here + k) % half
        d = base_near + s
        unit_copy(d, s, d, d, d, True).wait_send()
        return 0

    def drain_far(s, _):
        d = base_far + s
        unit_copy(d, s, d, d, d, False).wait_send()
        return 0

    lax.fori_loop(1, n, drain, 0)
    lax.fori_loop(1, half, drain_near, 0)
    lax.fori_loop(0, half, drain_far, 0)


def params(number):
    return pltpu.CompilerParams(
        collective_id=number, has_side_effects=True, vmem_limit_bytes=56 * 1024 * 1024
    )


def exchange(number, n, near, far, rows, width):
    half = n // 2
    tile = 2 if half * near <= 1024 else 1
    vmem = pl.BlockSpec(memory_space=pltpu.VMEM)
    dma = pltpu.SemaphoreType.DMA((n,))
    return pl.pallas_call(
        functools.partial(kernel, n, near, far, tile),
        out_shape=jax.ShapeDtypeStruct((1, rows), jnp.float32),
        in_specs=[vmem] * 5,
        out_specs=vmem,
        scratch_shapes=[
            pltpu.VMEM((n, LANES, width), jnp.bfloat16),
            pltpu.VMEM((half, near, width), jnp.bfloat16),
            pltpu.VMEM((half, far, width), jnp.bfloat16),
            pltpu.VMEM((n, 8, LANES), jnp.float32),
            pltpu.VMEM((n, 8, LANES), jnp.float32),
            pltpu.VMEM((half * near, LANES), jnp.float32),
            pltpu.VMEM((half * near, LANES), jnp.float32),
            pltpu.VMEM((half * far, LANES), jnp.float32),
            pltpu.VMEM((half * far, LANES), jnp.float32),
            pltpu.VMEM((8, half * near), jnp.float32),
            pltpu.VMEM((half * far, LANES), jnp.float32),
            pltpu.VMEM((n, 8, LANES), jnp.float32),
            pltpu.VMEM((n, 8, LANES), jnp.float32),
            dma, dma, dma, dma, dma, dma,
        ],
        compiler_params=params(number),
    )


def per_device(embeddings, owner_ids, local_cluster, arrival_rank):
    rows, width = embeddings.shape
    n = lax.axis_size("blk")
    groups = lax.axis_size("parts")
    vmem = pl.BlockSpec(memory_space=pltpu.VMEM)
    near = min(LANES, -(-7 * rows // (4 * n) // 16) * 16)
    far = min(LANES, -(-5 * rows // (4 * n) // 16) * 16)
    owner = owner_ids.reshape(1, rows)
    local = local_cluster.reshape(1, rows)
    rank = arrival_rank.reshape(1, rows)
    unit, target, most = pl.pallas_call(
        functools.partial(plan, n, groups, near, far),
        out_shape=(
            jax.ShapeDtypeStruct((rows, width), jnp.bfloat16),
            jax.ShapeDtypeStruct((1, rows), jnp.int32),
            jax.ShapeDtypeStruct((1, 1), jnp.float32),
        ),
        in_specs=[vmem] * 3,
        out_specs=(vmem, vmem, pl.BlockSpec(memory_space=pltpu.SMEM)),
        scratch_shapes=[
            pltpu.VMEM((n, n, LANES), jnp.float32),
            pltpu.VMEM((groups, 8, LANES), jnp.float32),
            pltpu.SemaphoreType.DMA((n,)),
            pltpu.SemaphoreType.DMA((n,)),
            pltpu.SemaphoreType.DMA((groups,)),
            pltpu.SemaphoreType.DMA((groups,)),
        ],
        compiler_params=params(0),
    )(embeddings, owner, local)
    scores = lax.cond(
        most[0, 0] <= 0.0,
        lambda: exchange(1, n, near, far, rows, width)(unit, target, owner, local, rank),
        lambda: exchange(2, n, LANES, LANES, rows, width)(unit, owner, owner, local, rank),
    )
    return scores.reshape(rows)


def solution(mesh):
    return jax.shard_map(
        per_device,
        mesh=mesh,
        in_specs=(
            P(("parts", "blk"), None),
            P(("parts", "blk"), None),
            P(("parts", "blk")),
            P(("parts", "blk")),
        ),
        out_specs=P(("parts", "blk")),
        check_vma=False,
    )
```
